32 devices in a mesh: coarse: 4 (over x, core), fine: 8 (over z, y).
Axes of the slice: x: 2, y: 2, z: 4, core: 2. Of those that a mesh axis runs over, the one named last changes fastest.
Arguments:
- tokens: bfloat16 [16384, 1024], P(('coarse', 'fine'))
- w_qkv: bfloat16 [1024, 3072], replicated, may hold values from -0.1875 to 0.1875
- w_coarse_out: bfloat16 [1024, 1024], replicated, may hold values from -0.1875 to 0.1875
- w_kv2: bfloat16 [1024, 2048], replicated, may hold values from -0.1875 to 0.1875
- w_out: bfloat16 [1024, 1024], replicated, may hold values from -0.1875 to 0.1875
- seg_start: int32 [512], P('coarse'), may hold values from 0 to 16383, as said below
- seg_end: int32 [512], P('coarse'), may hold values from 1 to 16384, as said below
- block_lists: int32 [64, 8], P(('coarse', 'fine')), may hold values from 0 to 31, as said below
Outputs:
- mixed: bfloat16 [16384, 1024], P(('coarse', 'fine'))
The draws below stay inside these ranges and needn't reach their ends.
Inputs may be any that keep to these rules, and one draw needn't show every extreme that they name: `seg_start`: for each coarse owner c, the segments c*128 to (c+1)*128 - 1 are nonempty and pairwise disjoint and lie within time steps c*4096 to (c+1)*4096 - 1, listed in an order that does not follow time; steps outside all segments belong to none; segment lengths are uneven. seg_end[s] > seg_start[s]. `block_lists`: row n names 8 distinct coarse key blocks (block b holds segments b*16 to (b+1)*16 - 1), all among the blocks of owners c-1, c and c+1 taken cyclically over the owners, where c = n*256 // 4096 is the owner of the row's time steps.
All inputs are finite; a program needn't handle non-finite values.
Results may differ from the reference program's by a relative error of at most 0.017.
Values may be sent and summed in bfloat16 or wider, within the bound.
No kernel may reach another device: no remote copies, remote signals or barrier semaphores. Data moves between devices by JAX's collectives and lax.ppermute only.
A program may use at most 128 MiB of HBM per device.

```python
import math
import jax
import jax.numpy as jnp
from jax import lax

D = 1024
HEADS = 8
TOK_DEV = 512
KB = 16
QB = 256
NBL = 8
STEP_COUNT_ALL = 16384
SPAN = 4096
SEG_OWN = 128
NSEG = 512
WC = 64
NQB = 64
N_COARSE = 4
N_FINE = 8


def segment_table(key):
    base_key = jax.random.fold_in(key, 7)
    owner_keys = jax.random.split(base_key, N_COARSE)

    def one_owner(owner_key):
        cut_key, trim_key, order_key = jax.random.split(owner_key, 3)
        shuffled = jax.random.permutation(cut_key, SPAN - 1).astype(jnp.int32)
        cuts = jnp.sort(shuffled[:SEG_OWN - 1] + 1)
        starts = jnp.concatenate([jnp.zeros((1,), jnp.int32), cuts])
        limits = jnp.concatenate([cuts, jnp.full((1,), SPAN, jnp.int32)])
        spans = limits - starts
        trims = jax.random.randint(trim_key, (SEG_OWN,), 0, spans // 2 + 1).astype(jnp.int32)
        ends = starts + spans - trims
        order = jax.random.permutation(order_key, SEG_OWN).astype(jnp.int32)
        return (jnp.take(starts, order), jnp.take(ends, order))
    starts, ends = jax.vmap(one_owner)(owner_keys)
    offsets = jnp.arange(N_COARSE, dtype=jnp.int32)[:, None] * SPAN
    return ((starts + offsets).reshape(NSEG), (ends + offsets).reshape(NSEG))


def draw_seg_start(key, part):
    return segment_table(key)[0]


def draw_seg_end(key, part):
    return segment_table(key)[1]


def draw_block_lists(key, part):
    choices_per_row = 3 * N_FINE
    scores = jax.random.randint(jax.random.fold_in(key, 11), (NQB, choices_per_row), 0, 1 << 20).astype(jnp.int32)
    scores = scores * choices_per_row + jnp.arange(choices_per_row, dtype=jnp.int32)[None, :]
    picks = jnp.argsort(scores, axis=1)[:, :NBL].astype(jnp.int32)
    owner = jnp.arange(NQB, dtype=jnp.int32) * QB // SPAN
    blocks = owner[:, None] * N_FINE - N_FINE + picks
    return jnp.mod(blocks, N_COARSE * N_FINE).astype(jnp.int32)


def draw_tokens(key, part):
    first_key = jax.random.fold_in(jax.random.fold_in(key, 3), 0)
    content_elements = jax.random.normal(first_key, (STEP_COUNT_ALL, D), jnp.float32)
    return jnp.clip(content_elements, -60.0, 60.0).astype(jnp.bfloat16)


def normal_values(key, dims, width, limit, kind=jnp.bfloat16):
    entries = jax.random.normal(key, dims, jnp.float32) * width
    return jnp.minimum(jnp.maximum(entries, -limit), limit).astype(kind)


def setup_inputs(seed: int = 0) -> dict:
    key_of = jax.random.split(jax.random.key(seed), 9)
    tokens = draw_tokens(jax.random.fold_in(key_of[8], 71), 0)
    w_qkv = normal_values(key_of[1], (D, 3 * D), D ** -0.5, 0.1875)
    w_coarse_out = normal_values(key_of[2], (D, D), D ** -0.5, 0.1875)
    w_kv2 = normal_values(key_of[3], (D, 2 * D), D ** -0.5, 0.1875)
    w_out = normal_values(key_of[4], (D, D), D ** -0.5, 0.1875)
    seg_start = draw_seg_start(jax.random.fold_in(key_of[8], 71), 0)
    seg_end = draw_seg_end(jax.random.fold_in(key_of[8], 71), 0)
    block_lists = draw_block_lists(jax.random.fold_in(key_of[8], 71), 0)
    return {"tokens": tokens, "w_qkv": w_qkv, "w_coarse_out": w_coarse_out, "w_kv2": w_kv2, "w_out": w_out, "seg_start": seg_start, "seg_end": seg_end, "block_lists": block_lists}


def attend_heads(queries, keys, content_elements, allowed):
    count = queries.shape[0]
    head_size = queries.shape[1] // HEADS
    query_heads = queries.astype(jnp.float32).reshape(count, HEADS, head_size)
    key_heads = keys.astype(jnp.float32).reshape(keys.shape[0], HEADS, head_size)
    value_heads = content_elements.astype(jnp.float32).reshape(content_elements.shape[0], HEADS, head_size)
    scores = jnp.einsum('qhd,khd->hqk', query_heads, key_heads) * (1.0 / math.sqrt(head_size))
    scores = jnp.where(allowed[None], scores, -1e+30)
    highest = lax.optimization_barrier(jnp.max(scores, axis=-1, keepdims=True))
    expos = jnp.exp(scores - highest)
    weights = (expos / lax.optimization_barrier(jnp.sum(expos, axis=-1, keepdims=True))).astype(jnp.bfloat16)
    blended = jnp.einsum('hqk,khd->qhd', weights.astype(jnp.float32), value_heads)
    return blended.astype(jnp.bfloat16).reshape(count, HEADS * head_size)

def normalize(content_elements):
    return content_elements * lax.rsqrt(lax.optimization_barrier(jnp.mean(content_elements * content_elements, axis=-1, keepdims=True)) + 1e-06)

def reference(tokens, w_qkv, w_coarse_out, w_kv2, w_out, seg_start, seg_end, block_lists):

    def pool_owner(owner):
        rows = lax.dynamic_slice_in_dim(tokens, owner * SPAN, SPAN, 0)
        starts = lax.dynamic_slice_in_dim(seg_start, owner * SEG_OWN, SEG_OWN, 0)
        ends = lax.dynamic_slice_in_dim(seg_end, owner * SEG_OWN, SEG_OWN, 0)
        places = owner * SPAN + jnp.arange(SPAN, dtype=jnp.int32)
        member = ((places[None, :] >= starts[:, None]) & (places[None, :] < ends[:, None])).astype(jnp.bfloat16)
        return jnp.dot(member, rows, preferred_element_type=jnp.float32)
    sums = lax.map(pool_owner, jnp.arange(N_COARSE, dtype=jnp.int32)).reshape(NSEG, D)
    spans = (seg_end - seg_start).astype(jnp.float32)
    pooled = (sums / jnp.sqrt(spans)[:, None]).astype(jnp.bfloat16)
    coarse_proj = jnp.dot(pooled, w_qkv, preferred_element_type=jnp.float32)
    coarse_query = coarse_proj[:, :D].astype(jnp.bfloat16)
    coarse_key = coarse_proj[:, D:2 * D].astype(jnp.bfloat16)
    coarse_value = coarse_proj[:, 2 * D:].astype(jnp.bfloat16)
    places = jnp.arange(NSEG, dtype=jnp.int32)
    apart = jnp.abs(places[:, None] - places[None, :])
    allowed = jnp.minimum(apart, NSEG - apart) <= WC
    coarse_mix = attend_heads(coarse_query, coarse_key, coarse_value, allowed)
    context = jnp.dot(coarse_mix, w_coarse_out, preferred_element_type=jnp.float32)
    state = normalize(context).astype(jnp.bfloat16)
    second = jnp.dot(state, w_kv2, preferred_element_type=jnp.float32).astype(jnp.bfloat16)
    per_device = TOK_DEV // QB

    def device_rows(device):
        rows = lax.dynamic_slice_in_dim(tokens, device * TOK_DEV, TOK_DEV, 0)
        proj = jnp.dot(rows, w_qkv, preferred_element_type=jnp.float32)
        query = proj[:, :D].astype(jnp.bfloat16)
        key_rows = proj[:, D:2 * D].astype(jnp.bfloat16)
        value_rows = proj[:, 2 * D:].astype(jnp.bfloat16)
        lists = lax.dynamic_slice_in_dim(block_lists, device * per_device, per_device, 0)

        def query_block(number):
            block_query = lax.dynamic_slice_in_dim(query, number * QB, QB, 0)
            listed = lax.dynamic_index_in_dim(lists, number, 0, keepdims=False)
            picked = (listed[:, None] * KB + jnp.arange(KB, dtype=jnp.int32)[None, :]).reshape(-1)
            remote = jnp.take(second, picked, axis=0)
            keys = jnp.concatenate([key_rows, remote[:, :D]], axis=0)
            content_elements = jnp.concatenate([value_rows, remote[:, D:]], axis=0)
            allowed_all = jnp.ones((QB, keys.shape[0]), dtype=bool)
            return attend_heads(block_query, keys, content_elements, allowed_all)
        attended = lax.map(query_block, jnp.arange(per_device, dtype=jnp.int32)).reshape(TOK_DEV, D)
        projected = jnp.dot(attended, w_out, preferred_element_type=jnp.float32)
        return normalize(projected).astype(jnp.bfloat16)
    mixed = lax.map(device_rows, jnp.arange(N_COARSE * N_FINE, dtype=jnp.int32))
    return mixed.reshape(STEP_COUNT_ALL, D)
```

```python
import functools
import math

import jax
import jax.numpy as jnp
from jax import lax
from jax.experimental import pallas as pl
from jax.experimental.pallas import tpu as pltpu
from jax.sharding import PartitionSpec as P

HEADS = 8
KB = 16
QB = 256
BLK = 128
MIB = 1 << 20
AXES = ("coarse", "fine")
F32 = jnp.float32
BF16 = jnp.bfloat16

VM = pl.BlockSpec(memory_space=pltpu.VMEM)
SM = pl.BlockSpec(memory_space=pltpu.SMEM)


def cdiv(a, b):
    return -(-a // b)


def dot(a, b):
    return jnp.dot(a, b, preferred_element_type=F32)


def dot_t(a, b):
    return lax.dot_general(a, b, (((1,), (1,)), ((), ())), preferred_element_type=F32)


def call(kernel, outs, in_specs, scratch, limit, flops, moved, name):
    return pl.pallas_call(
        kernel,
        out_shape=outs,
        in_specs=in_specs,
        out_specs=jax.tree.map(lambda _: VM, outs),
        scratch_shapes=scratch,
        compiler_params=pltpu.CompilerParams(vmem_limit_bytes=limit * MIB),
        cost_estimate=pl.CostEstimate(flops=flops, bytes_accessed=moved, transcendentals=0),
        name=name,
    )


def sums_kernel(chunk, place, starts, ends, tokens, own, send, acc):
    rows = tokens.shape[0]
    owned = starts.shape[1]
    mine = place[0]
    first = place[1]
    where_ = first + lax.broadcasted_iota(jnp.int32, (BLK, rows), 1)
    for s in range(owned // BLK):
        at = slice(s * BLK, (s + 1) * BLK)
        low = jnp.broadcast_to(starts[:, at], (BLK, BLK)).T
        high = jnp.broadcast_to(ends[:, at], (BLK, BLK)).T
        low = jnp.concatenate([low] * (rows // BLK), axis=1)
        high = jnp.concatenate([high] * (rows // BLK), axis=1)
        member = jnp.where((where_ >= low) & (where_ < high), 1.0, 0.0).astype(BF16)
        acc[at, :] = dot(member, tokens[...])
    own[...] = acc[pl.ds(pl.multiple_of(mine * chunk, chunk), chunk), :]
    for r in range(1, 4):
        theirs = pl.multiple_of((mine ^ r) * chunk, chunk)
        send[r - 1] = acc[pl.ds(theirs, chunk), :].astype(BF16)


def local_kernel(first, heads, size, scale, tokens, w_qkv, query, mix, level):
    width = tokens.shape[1]
    span = heads * size
    parts = []
    for k in range(3):
        at = k * width + first * size
        parts.append(dot(tokens[...], w_qkv[:, at : at + span]).astype(BF16))
    queries, keys, cells = parts
    query[...] = queries
    ones = jnp.ones((keys.shape[0], size), BF16)
    for i in range(heads):
        at = slice(i * size, (i + 1) * size)
        scores = dot_t(queries[:, at], keys[:, at])
        highest = jnp.max(scores, axis=1, keepdims=True)
        expos = jnp.exp2((scores - highest) * scale).astype(BF16)
        both = dot(expos, jnp.concatenate([cells[:, at], ones], axis=1))
        total = both[:, size:]
        mix[:, at] = both[:, :size] / total
        level[:, at] = highest * scale + jnp.log2(total)


def normalize_rows(source, target):
    def step(i, carry):
        at = pl.ds(pl.multiple_of(i * BLK, BLK), BLK)
        cells = source[at, :]
        level = jnp.mean(cells * cells, axis=1, keepdims=True)
        target[at, :] = (cells * lax.rsqrt(level + 1e-06)).astype(BF16)
        return carry

    lax.fori_loop(0, source.shape[0] // BLK, step, 0)


def matmul_into(target, source, weight, first, count, tile):
    def step(i, carry):
        to = pl.ds(pl.multiple_of(i * tile, tile), tile)
        of = pl.ds(pl.multiple_of(first + i * tile, tile), tile)
        target[:, to] = dot(source[...], weight[:, of]).astype(target.dtype)
        return carry

    lax.fori_loop(0, count // tile, step, 0)


def final_kernel(
    chunk, reach, size, scale, total_rows, group,
    place, lists, own0, own1, before0, before1, after0, after1, pair0, pair1, side0, side1,
    w_qkv, w_co, w_kv2, w_out, *rest,
):
    parts = len(rest) - 8
    query, mix, level = (rest[k:parts:3] for k in range(3))
    out, table, halo, pairs, coarse, wide, listed, second = rest[parts:]
    width = table.shape[1]
    owned = chunk * 4
    mine = place[0]
    core = place[2]
    owner = place[3]

    def lay(base, zero, one):
        for r in range(4):
            to = pl.multiple_of(base + (mine ^ r) * chunk, chunk)
            source = one if r & 1 else zero
            table[pl.ds(to, chunk), :] = source[(r >> 1) * chunk : (r >> 1) * chunk + chunk, :]

    def lay_halo(zero, one, first, to):
        for r in range(4):
            at = pl.multiple_of((mine ^ r) * chunk, chunk)
            source = one if r & 1 else zero
            halo[pl.ds(at, chunk), :] = source[(r >> 1) * chunk : (r >> 1) * chunk + chunk, :]
        table[to : to + reach, :] = halo[first : first + reach, :]

    lay_halo(before0, before1, owned - reach, 0)
    lay_halo(after0, after1, 0, reach + 3 * owned)
    lay(reach + owned, own0, own1)
    lay(reach + (1 - core) * 2 * owned, pair0, pair1)
    lay(reach + core * 2 * owned, side0, side1)

    matmul_into(pairs, table, w_qkv, width, 2 * width, 512)
    matmul_into(coarse, table.at[pl.ds(reach, 3 * owned)], w_qkv, 0, width, 512)

    span = BLK + 2 * reach
    row = lax.broadcasted_iota(jnp.int32, (BLK, span), 0)
    column = lax.broadcasted_iota(jnp.int32, (BLK, span), 1)
    inside = (column >= row) & (column <= row + 2 * reach)
    ones = jnp.ones((span, size), BF16)

    def coarse_step(i, carry):
        first = pl.multiple_of(i * BLK, BLK)
        for h in range(HEADS):
            at = slice(h * size, (h + 1) * size)
            keys = pairs[pl.ds(first, span), at]
            cells = pairs[pl.ds(first, span), width + h * size : width + (h + 1) * size]
            scores = jnp.where(inside, dot_t(coarse[pl.ds(first, BLK), at], keys), -1e30)
            highest = jnp.max(scores, axis=1, keepdims=True)
            expos = jnp.exp2((scores - highest) * scale).astype(BF16)
            both = dot(expos, jnp.concatenate([cells, ones], axis=1))
            coarse[pl.ds(first, BLK), at] = (both[:, :size] / both[:, size:]).astype(BF16)
        return carry

    lax.fori_loop(0, 3 * owned // BLK, coarse_step, 0)
    matmul_into(wide.at[pl.ds(0, 3 * owned)], coarse, w_co, 0, width, 512)
    normalize_rows(wide.at[pl.ds(0, 3 * owned)], coarse)

    base = (owner - 1) * owned
    groups, picks = lists.shape
    for n in range(groups):
        for m in range(picks):
            at = lax.rem(lists[n, m] * KB - base + total_rows, total_rows)
            to = (n * picks + m) * KB
            listed[to : to + KB, :] = coarse[pl.ds(pl.multiple_of(at, KB), KB), :]
    matmul_into(second, listed, w_kv2, 0, 2 * width, 512)

    here = picks * KB
    ones_here = jnp.ones((here, size), BF16)
    for n in range(groups):
        rows = slice(n * QB, (n + 1) * QB)
        theirs = slice(n * here, (n + 1) * here)
        for h in range(HEADS):
            at = slice(h * size, (h + 1) * size)
            part, where_ = h // group, slice(h % group * size, (h % group + 1) * size)
            scores = dot_t(query[part][rows, where_], second[theirs, at]) * scale
            before = level[part][rows, where_]
            highest = jnp.maximum(before, jnp.max(scores, axis=1, keepdims=True))
            expos = jnp.exp2(scores - highest[:, :here]).astype(BF16)
            cells = second[theirs, width + h * size : width + (h + 1) * size]
            both = dot(expos, jnp.concatenate([cells, ones_here], axis=1))
            keep = jnp.exp2(before - highest)
            mixed = mix[part][rows, where_] * keep + both[:, :size]
            out[rows, at] = (mixed / (keep + both[:, size:])).astype(BF16)
    rows_here = out.shape[0]
    matmul_into(wide.at[pl.ds(0, rows_here)], out, w_out, 0, width, 512)
    normalize_rows(wide.at[pl.ds(0, rows_here)], out)


def swap(cells, coarse_bit, fine_bit):
    coarse_count = lax.axis_size("coarse")
    fine_count = lax.axis_size("fine")
    pairs = [
        (c * fine_count + f, (c ^ coarse_bit) * fine_count + (f ^ fine_bit))
        for c in range(coarse_count)
        for f in range(fine_count)
    ]
    return lax.ppermute(cells, AXES, pairs)


def shift(cells, chips, fine_bit):
    coarse_count = lax.axis_size("coarse")
    fine_count = lax.axis_size("fine")
    pairs = [
        (c * fine_count + f, ((c + 2 * chips) % coarse_count) * fine_count + (f ^ fine_bit))
        for c in range(coarse_count)
        for f in range(fine_count)
    ]
    return lax.ppermute(cells, AXES, pairs)


def body(tokens, w_qkv, w_coarse_out, w_kv2, w_out, seg_start, seg_end, block_lists):
    rows_here, width = tokens.shape
    size = width // HEADS
    fine_count = lax.axis_size("fine")
    coarse_count = lax.axis_size("coarse")
    fine_index = lax.axis_index("fine")
    coarse_index = lax.axis_index("coarse")
    owned = seg_start.shape[0]
    chunk = owned // 4
    reach = owned // 2
    scale = math.log2(math.e) / math.sqrt(size)
    mine = fine_index & 3
    big = coarse_count > 4
    if not big:
        tokens, w_qkv, w_coarse_out, w_kv2, w_out = (
            pltpu.with_memory_space_constraint(c, pltpu.VMEM)
            for c in (tokens, w_qkv, w_coarse_out, w_kv2, w_out)
        )
    first_row = coarse_index * (rows_here * fine_count) + fine_index * rows_here
    place = jnp.stack([mine, first_row, coarse_index & 1, coarse_index]).astype(jnp.int32)

    own, send = call(
        functools.partial(sums_kernel, chunk),
        (
            jax.ShapeDtypeStruct((chunk, width), F32),
            jax.ShapeDtypeStruct((3, chunk, width), BF16),
        ),
        [SM, VM, VM, VM],
        [pltpu.VMEM((owned, width), F32)],
        16,
        2 * owned * rows_here * width,
        rows_here * width * 2,
        "sums",
    )(place, seg_start.reshape(1, owned), seg_end.reshape(1, owned), tokens)

    group = 2

    def local(first):
        span = group * size
        return call(
            functools.partial(local_kernel, first, group, size, scale),
            (
                jax.ShapeDtypeStruct((rows_here, span), BF16),
                jax.ShapeDtypeStruct((rows_here, span), F32),
                jax.ShapeDtypeStruct((rows_here, span), F32),
            ),
            [VM, VM],
            [],
            32 if big else 16,
            2 * rows_here * width * 3 * span,
            width * 3 * span * 2,
            f"local{first}",
        )(tokens, w_qkv)

    parts = [part for first in range(0, HEADS, group) for part in local(first)]

    spans = (
        lax.dynamic_slice_in_dim(seg_end, mine * chunk, chunk, 0)
        - lax.dynamic_slice_in_dim(seg_start, mine * chunk, chunk, 0)
    ).astype(F32)
    roots = jnp.sqrt(spans)[:, None]

    got = [swap(send[r - 1], 0, r) for r in range(1, 4)]
    sums = own + got[0].astype(F32) + got[1].astype(F32) + got[2].astype(F32)
    bit = 4
    while bit < fine_count:
        sums = sums + swap(sums.astype(BF16), 0, bit).astype(F32)
        bit *= 2
    pooled = (sums / roots).astype(BF16)
    own0 = jnp.concatenate([pooled, swap(pooled, 0, 2)], axis=0)
    own1 = swap(own0, 0, 1)
    chips = coarse_count // 2
    core = coarse_index & 1
    if chips == 2:
        before0 = after0 = side0 = swap(own0, 2, 0)
        before1 = after1 = side1 = swap(own0, 2, 1)
    else:
        before0, before1 = shift(own0, 1, 0), shift(own0, 1, 1)
        after0, after1 = shift(own0, -1, 0), shift(own0, -1, 1)
        side0 = jnp.where(core == 0, after0, before0)
        side1 = jnp.where(core == 0, after1, before1)
    pair0, pair1, side0, side1 = (swap(c, 1, 0) for c in (own0, own1, side0, side1))

    table_rows = 3 * owned + 2 * reach
    listed_rows = block_lists.shape[0] * block_lists.shape[1] * KB
    wide_rows = max(rows_here, 3 * owned)
    return call(
        functools.partial(final_kernel, chunk, reach, size, scale, owned * coarse_count, group),
        jax.ShapeDtypeStruct((rows_here, width), BF16),
        [SM, SM] + [VM] * (14 + len(parts)),
        [
            pltpu.VMEM((table_rows, width), BF16),
            pltpu.VMEM((owned, width), BF16),
            pltpu.VMEM((table_rows, 2 * width), BF16),
            pltpu.VMEM((3 * owned, width), BF16),
            pltpu.VMEM((wide_rows, width), F32),
            pltpu.VMEM((listed_rows, width), BF16),
            pltpu.VMEM((listed_rows, 2 * width), BF16),
        ],
        60 if big else 20,
        2 * table_rows * width * 3 * width,
        0,
        "final",
    )(
        place, block_lists, own0, own1, before0, before1, after0, after1, pair0, pair1, side0, side1,
        w_qkv, w_coarse_out, w_kv2, w_out, *parts,
    )


def solution(mesh):
    placed = (
        P(("coarse", "fine"), None),
        P(),
        P(),
        P(),
        P(),
        P("coarse"),
        P("coarse"),
        P(("coarse", "fine"), None),
    )
    return jax.shard_map(
        body, mesh=mesh, in_specs=placed, out_specs=P(("coarse", "fine"), None), check_vma=False
    )
```

```python
import functools
import math

import jax
import jax.numpy as jnp
from jax import lax
from jax.experimental import pallas as pl
from jax.experimental.pallas import tpu as pltpu
from jax.sharding import PartitionSpec as P

HEADS = 8
KB = 16
QB = 256
BLK = 128
MIB = 1 << 20
AXES = ("coarse", "fine")
F32 = jnp.float32
BF16 = jnp.bfloat16

VM = pl.BlockSpec(memory_space=pltpu.VMEM)
SM = pl.BlockSpec(memory_space=pltpu.SMEM)
ANY = pl.BlockSpec(memory_space=pl.ANY)
FAR = pl.BlockSpec(memory_space=pltpu.HBM)


def cdiv(a, b):
    return -(-a // b)


def dot(a, b):
    return jnp.dot(a, b, preferred_element_type=F32)


def dot_t(a, b):
    return lax.dot_general(a, b, (((1,), (1,)), ((), ())), preferred_element_type=F32)


def call(kernel, outs, in_specs, scratch, limit, flops, moved, name, out_specs=None):
    return pl.pallas_call(
        kernel,
        out_shape=outs,
        in_specs=in_specs,
        out_specs=out_specs or jax.tree.map(lambda _: VM, outs),
        scratch_shapes=scratch,
        compiler_params=pltpu.CompilerParams(vmem_limit_bytes=limit * MIB),
        cost_estimate=pl.CostEstimate(flops=flops, bytes_accessed=moved, transcendentals=0),
        name=name,
    )


def sums_kernel(chunk, place, starts_far, ends_far, tokens_far, own, send, tokens, roots, acc, root, starts, ends, sem):
    copies = [
        pltpu.make_async_copy(source, target, sem.at[i])
        for i, (source, target) in enumerate(((starts_far, starts), (ends_far, ends), (tokens_far, tokens)))
    ]
    for copy in copies:
        copy.start()
    rows = tokens.shape[0]
    owned = starts.shape[1]
    mine = place[0]
    where_ = place[1] + lax.broadcasted_iota(jnp.int32, (BLK, rows), 1)
    copies[0].wait()
    copies[1].wait()
    members = []
    for s in range(owned // BLK):
        at = slice(s * BLK, (s + 1) * BLK)
        low = jnp.broadcast_to(starts[:, at], (BLK, BLK)).T
        high = jnp.broadcast_to(ends[:, at], (BLK, BLK)).T
        root[at, :] = jnp.sqrt((high - low).astype(F32))
        low = jnp.concatenate([low] * (rows // BLK), axis=1)
        high = jnp.concatenate([high] * (rows // BLK), axis=1)
        members.append(jnp.where((where_ >= low) & (where_ < high), 1.0, 0.0).astype(BF16))
    copies[2].wait()
    for s in range(owned // BLK):
        acc[s * BLK : (s + 1) * BLK, :] = dot(members[s], tokens[...])
    own[...] = acc[pl.ds(pl.multiple_of(mine * chunk, chunk), chunk), :]
    for i, r in enumerate((0, 2)):
        roots[i * chunk : (i + 1) * chunk, :] = root[pl.ds(pl.multiple_of((mine ^ r) * chunk, chunk), chunk), :]
    for r in range(1, 4):
        theirs = pl.multiple_of((mine ^ r) * chunk, chunk)
        send[r - 1][...] = acc[pl.ds(theirs, chunk), :].astype(BF16)


def add_kernel(own, *rest):
    *got, total, half = rest
    sums = own[...]
    for cells in got:
        sums = sums + cells[...].astype(F32)
    total[...] = sums
    half[...] = sums.astype(BF16)


def pool_kernel(total, across, beside, corner, roots, pooled):
    chunk, width = total.shape
    mine = total[...] + across[...].astype(F32)
    theirs = beside[...].astype(F32) + corner[...].astype(F32)
    root = jnp.concatenate([roots[...]] * (width // BLK), axis=1)
    pooled[:chunk, :] = (mine / root[:chunk]).astype(BF16)
    pooled[chunk:, :] = (theirs / root[chunk:]).astype(BF16)


def local_kernel(first, heads, size, scale, tokens, weights, after, query, mix, level):
    del after
    width = tokens.shape[1]
    span = heads * size
    parts = [
        dot(tokens[...], weights[:, k * width + first * size : k * width + first * size + span]).astype(BF16)
        for k in range(3)
    ]
    attend_here(heads, size, scale, parts, query, mix, level)


def far_kernel(first, heads, size, scale, tokens, w_far, after, query, mix, level, weights, sem):
    del after
    width = tokens.shape[1]
    span = heads * size
    copies = []
    for k in range(3):
        at = k * width + first * size
        copies.append(pltpu.make_async_copy(w_far.at[:, at : at + span], weights.at[k], sem.at[k]))
        copies[k].start()
    parts = []
    for k in range(3):
        copies[k].wait()
        parts.append(dot(tokens[...], weights[k]).astype(BF16))
    attend_here(heads, size, scale, parts, query, mix, level)


def attend_here(heads, size, scale, parts, query, mix, level):
    queries, keys, cells = parts
    query[...] = queries
    ones = jnp.ones((keys.shape[0], size), BF16)
    for i in range(heads):
        at = slice(i * size, (i + 1) * size)
        scores = dot_t(queries[:, at], keys[:, at])
        highest = jnp.max(scores, axis=1, keepdims=True)
        expos = jnp.exp2((scores - highest) * scale).astype(BF16)
        both = dot(expos, jnp.concatenate([cells[:, at], ones], axis=1))
        total = both[:, size:]
        mix[:, at] = both[:, :size] / total
        level[:, at] = highest * scale + jnp.log2(total)


def normalize(cells):
    return cells * lax.rsqrt(jnp.mean(cells * cells, axis=1, keepdims=True) + 1e-06)


def rows_kernel(cells, w_qkv, out):
    for c in range(0, out.shape[1], 512):
        out[:, c : c + 512] = dot(cells[...], w_qkv[:, c : c + 512]).astype(BF16)


def move(chunk, cells, targets):
    for i, (target, to, columns) in enumerate(targets):
        target[pl.ds(pl.multiple_of(to, chunk), chunk), columns] = cells[i * chunk : (i + 1) * chunk, :]


def near_kernel(chunk, place, own1, ends0, ends1, done, w_qkv, pairs):
    width = w_qkv.shape[0]
    owned = chunk * 4
    mine = place[0]
    cells = jnp.concatenate([own1[...], ends0[...], ends1[...]], axis=0)
    at = [(mine ^ r) * chunk for r in (1, 3)]
    at += [owned + (mine ^ r ^ 2) * chunk for r in (0, 2, 1, 3)]
    for c in range(0, 2 * width, 512):
        columns = slice(c, c + 512)
        found = dot(cells, w_qkv[:, width + c : width + c + 512]).astype(BF16)
        move(chunk, found, [(pairs, to, columns) for to in at])
    before = [mine * chunk, (mine ^ 2) * chunk]
    move(chunk, done[:, width:], [(pairs, to, slice(None)) for to in before])


def final_kernel(
    chunk, reach, size, scale, total_rows, head_groups,
    place, lists, own1, pair0, pair1, side0, side1, done, near_pairs,
    w_qkv, w_co, w_kv2, w_out, *rest,
):
    parts = len(rest) - 8
    held = [(p, i) for p, count in enumerate(head_groups) for i in range(count)]
    query, mix, level = (rest[k:parts:3] for k in range(3))
    out, far_pairs, coarse_query, state, listed, attended, ready, sem = rest[parts:]
    width = state.shape[1]
    owned = chunk * 4
    mine = place[0]
    core = place[2]
    owner = place[3]

    own_at = [owned + (mine ^ r) * chunk for r in (0, 2, 1, 3)]
    pair_at = [(1 - core) * owned + (mine ^ r) * chunk for r in (0, 2, 1, 3)]
    side_at = [core * owned + (mine ^ r) * chunk for r in (0, 2, 1, 3)]
    pair_to = [(1 - core) * 2 * owned + (mine ^ r) * chunk for r in (0, 2, 1, 3)]
    side_to = [core * 2 * owned + (mine ^ r) * chunk for r in (0, 2, 1, 3)]
    rows = jnp.concatenate([pair0[...], pair1[...], side0[...], side1[...], own1[...]], axis=0)
    for c in range(0, width, 512):
        found = dot(rows, w_qkv[:, c : c + 512]).astype(BF16)
        move(chunk, found, [(coarse_query, to, slice(c, c + 512)) for to in pair_to + side_to + own_at[2:]])
    rows = rows[: 8 * chunk]
    for c in range(0, 2 * width, 512):
        found = dot(rows, w_qkv[:, width + c : width + c + 512]).astype(BF16)
        move(chunk, found, [(far_pairs, to, slice(c, c + 512)) for to in pair_at + side_at])
    move(chunk, done[:, :width], [(coarse_query, to, slice(None)) for to in own_at[:2]])

    runs = (
        (near_pairs, owned, reach),
        (far_pairs, 0, owned),
        (near_pairs, 0, owned),
        (far_pairs, owned, owned),
        (near_pairs, owned + reach, reach),
    )

    def window(first, count, columns):
        cells = []
        start = 0
        for source, at, rows in runs:
            low, high = max(first, start), min(first + count, start + rows)
            if low < high:
                cells.append(source[at + low - start : at + high - start, columns])
            start += rows
        return jnp.concatenate(cells, axis=0)

    span = BLK + 2 * reach
    row = lax.broadcasted_iota(jnp.int32, (BLK, span), 0)
    column = lax.broadcasted_iota(jnp.int32, (BLK, span), 1)
    inside = (column >= row) & (column <= row + 2 * reach)
    ones = jnp.ones((span, size), BF16)
    for first in range(0, 3 * owned, BLK):
        heads = [slice(h * size, (h + 1) * size) for h in range(HEADS)]
        scores = []
        for at in heads:
            score = dot_t(coarse_query[first : first + BLK, at], window(first, span, at))
            scores.append(jnp.where(inside, score, -1e30))
        tops = [jnp.max(score, axis=1, keepdims=True) for score in scores]
        expos = [jnp.exp2((score - top) * scale).astype(BF16) for score, top in zip(scores, tops)]
        mixed = []
        for at, expo in zip(heads, expos):
            cells = window(first, span, slice(width + at.start, width + at.stop))
            both = dot(expo, jnp.concatenate([cells, ones], axis=1))
            mixed.append((both[:, :size] / both[:, size:]).astype(BF16))
        context = dot(jnp.concatenate(mixed, axis=1), w_co[...])
        state[first : first + BLK, :] = normalize(context).astype(BF16)

    base = (owner - 1) * owned
    groups, picks = lists.shape
    for n in range(groups):
        for m in range(picks):
            at = lax.rem(lists[n, m] * KB - base + total_rows, total_rows)
            to = (n * picks + m) * KB
            listed[to : to + KB, :] = state[pl.ds(pl.multiple_of(at, KB), KB), :]
    here = picks * KB
    ones_here = jnp.ones((here, size), BF16)
    span2 = 2 * size
    second = [
        [dot(listed[...], w_kv2[:, k * width + c : k * width + c + span2]).astype(BF16) for k in range(2)]
        for c in range(0, width, span2)
    ]

    def fine(units):
        kept = []
        for n, h in units:
            part, place_in = held[h]
            at = slice(place_in * size, (place_in + 1) * size)
            keys, cells = (c[n * here : (n + 1) * here, h % 2 * size : (h % 2 + 1) * size] for c in second[h // 2])
            rows = slice(n * QB, (n + 1) * QB)
            kept.append((part, rows, at, cells, dot_t(query[part][rows, at], keys) * scale))
        tops = [
            jnp.maximum(level[part][rows, at], jnp.max(scores, axis=1, keepdims=True))
            for part, rows, at, cells, scores in kept
        ]
        boths = []
        for (part, rows, at, cells, scores), top in zip(kept, tops):
            expos = jnp.exp2(scores - top[:, :here]).astype(BF16)
            boths.append(dot(expos, jnp.concatenate([cells, ones_here], axis=1)))
        for (n, h), (part, rows, at, cells, scores), top, both in zip(units, kept, tops, boths):
            keep = jnp.exp2(level[part][rows, at] - top)
            mixed = mix[part][rows, at] * keep + both[:, :size]
            attended[rows, h * size : (h + 1) * size] = (mixed / (keep + both[:, size:])).astype(BF16)

    units = [(n, h) for h in range(HEADS) for n in range(groups)]
    for u in range(0, len(units), 8):
        fine(units[u : u + 8])
    copies = []
    for first in range(0, out.shape[0], BLK):
        some = slice(first, first + BLK)
        ready[some, :] = normalize(dot(attended[some, :], w_out[...])).astype(BF16)
        copies.append(pltpu.make_async_copy(ready.at[some], out.at[some], sem.at[len(copies)]))
        copies[-1].start()
    for copy in copies:
        copy.wait()


def swap(cells, coarse_bit, fine_bit):
    coarse_count = lax.axis_size("coarse")
    fine_count = lax.axis_size("fine")
    pairs = [
        (c * fine_count + f, (c ^ coarse_bit) * fine_count + (f ^ fine_bit))
        for c in range(coarse_count)
        for f in range(fine_count)
    ]
    return lax.ppermute(cells, AXES, pairs)


def shift(cells, chips, fine_bit):
    coarse_count = lax.axis_size("coarse")
    fine_count = lax.axis_size("fine")
    pairs = [
        (c * fine_count + f, ((c + 2 * chips) % coarse_count) * fine_count + (f ^ fine_bit))
        for c in range(coarse_count)
        for f in range(fine_count)
    ]
    return lax.ppermute(cells, AXES, pairs)


def body(tokens, w_qkv, w_coarse_out, w_kv2, w_out, seg_start, seg_end, block_lists):
    rows_here, width = tokens.shape
    size = width // HEADS
    fine_count = lax.axis_size("fine")
    coarse_count = lax.axis_size("coarse")
    fine_index = lax.axis_index("fine")
    coarse_index = lax.axis_index("coarse")
    owned = seg_start.shape[0]
    chunk = owned // 4
    reach = owned // 2
    scale = math.log2(math.e) / math.sqrt(size)
    mine = fine_index & 3
    big = coarse_count > 4
    far = functools.partial(pltpu.with_memory_space_constraint, memory_space=pltpu.HBM)
    kept = jax.ShapeDtypeStruct if big else pltpu.VMEM
    near = (lambda c: c) if big else functools.partial(pltpu.with_memory_space_constraint, memory_space=pltpu.VMEM)
    first_row = coarse_index * (rows_here * fine_count) + fine_index * rows_here
    place = jnp.stack([mine, first_row, coarse_index & 1, coarse_index]).astype(jnp.int32)

    own, *send, tokens, roots = call(
        lambda *refs: sums_kernel(chunk, *refs[:4], refs[4], refs[5:8], *refs[8:]),
        (
            jax.ShapeDtypeStruct((chunk, width), F32),
            *[jax.ShapeDtypeStruct((chunk, width), BF16)] * 3,
            kept(tokens.shape, BF16),
            jax.ShapeDtypeStruct((2 * chunk, BLK), F32),
        ),
        [SM, FAR, FAR, FAR],
        [
            pltpu.VMEM((owned, width), F32),
            pltpu.VMEM((owned, BLK), F32),
            pltpu.VMEM((1, owned), jnp.int32),
            pltpu.VMEM((1, owned), jnp.int32),
            pltpu.SemaphoreType.DMA((3,)),
        ],
        24 if big else 8,
        2 * owned * rows_here * width,
        rows_here * width * 2,
        "sums",
    )(place, far(seg_start.reshape(1, owned)), far(seg_end.reshape(1, owned)), far(tokens))

    head_groups = (2, 2, 4)

    def local(first, heads, weights, after):
        span = heads * size
        results = (
            jax.ShapeDtypeStruct((rows_here, span), BF16),
            jax.ShapeDtypeStruct((rows_here, span), F32),
            jax.ShapeDtypeStruct((rows_here, span), F32),
        )
        cost = 2 * rows_here * width * 3 * span, 0, f"local{first}"
        if first + heads < HEADS:
            return call(
                functools.partial(far_kernel, first, heads, size, scale),
                results,
                [VM, FAR, ANY],
                [pltpu.VMEM((3, width, span), BF16), pltpu.SemaphoreType.DMA((3,))],
                24 if big else 10,
                *cost,
            )(tokens, far(weights), after)
        kernel = functools.partial(local_kernel, first, heads, size, scale)
        return call(kernel, results, [VM, VM, ANY], [], 24 if big else 10, *cost)(tokens, weights, after)

    def beside(value, made):
        value, first = lax.optimization_barrier((value, made[0]))
        return value, [first, *made[1:]]

    got = [swap(send[r - 1], 0, r) for r in range(1, 4)]
    own, part = beside(own, local(0, 2, w_qkv, send[0]))
    parts = list(part)
    rows32 = jax.ShapeDtypeStruct((chunk, width), F32)
    rows16 = jax.ShapeDtypeStruct((chunk, width), BF16)

    def add(total, got):
        return call(
            add_kernel, (rows32, rows16), [VM] * (1 + len(got)), [], 8 if big else 4, 0, chunk * width, "add"
        )(total, *got)

    sums, half = add(own, got)
    bit = 8
    while bit < fine_count:
        sums, half = add(sums, [swap(half, 0, bit)])
        bit *= 2
    across, beside_half, corner = (swap(half, 0, bit) for bit in (4, 2, 6))
    sums, part = beside(sums, local(2, 2, w_qkv, half))
    parts.extend(part)
    own0 = call(
        pool_kernel,
        jax.ShapeDtypeStruct((2 * chunk, width), BF16),
        [VM] * 5,
        [],
        8 if big else 4,
        0,
        chunk * width,
        "pool",
    )(sums, across, beside_half, corner, roots)
    own1 = swap(own0, 0, 1)
    chips = coarse_count // 2
    core = coarse_index & 1
    if chips == 2:
        ends0 = side0 = swap(own0, 2, 0)
        ends1 = side1 = swap(own0, 2, 1)
    else:
        before0, before1 = shift(own0, 1, 0), shift(own0, 1, 1)
        after0, after1 = shift(own0, -1, 0), shift(own0, -1, 1)
        side0 = jnp.where(core == 0, after0, before0)
        side1 = jnp.where(core == 0, after1, before1)
        upper = jnp.repeat(jnp.stack([mine >= 2, mine < 2]), chunk)[:, None]
        ends0 = jnp.where(upper, before0, after0)
        ends1 = jnp.where(upper, before1, after1)
    done = call(
        rows_kernel,
        jax.ShapeDtypeStruct((2 * chunk, 3 * width), BF16),
        [VM, VM],
        [],
        40 if big else 8,
        2 * 2 * chunk * width * 3 * width,
        0,
        "rows",
    )(own0, w_qkv)
    side0, part = beside(side0, local(4, 4, w_qkv, own0))
    side0, (done,) = beside(side0, [done])
    own0 = lax.optimization_barrier((own0, side0))[0]
    parts.extend(part)
    pair0, pair1, side0, side1 = (swap(c, 1, 0) for c in (own0, own1, side0, side1))
    near_pairs = call(
        functools.partial(near_kernel, chunk),
        jax.ShapeDtypeStruct((2 * owned, 2 * width), BF16),
        [SM] + [VM] * 5,
        [],
        40 if big else 8,
        2 * owned * width * 3 * width,
        0,
        "near",
    )(place, own1, ends0, ends1, done, w_qkv)

    listed_rows = block_lists.shape[0] * block_lists.shape[1] * KB
    return call(
        functools.partial(final_kernel, chunk, reach, size, scale, owned * coarse_count, head_groups),
        jax.ShapeDtypeStruct((rows_here, width), BF16),
        [SM, SM] + [VM] * (11 + len(parts)),
        [
            pltpu.VMEM((2 * owned, 2 * width), BF16),
            pltpu.VMEM((3 * owned, width), BF16),
            pltpu.VMEM((3 * owned, width), BF16),
            pltpu.VMEM((listed_rows, width), BF16),
            pltpu.VMEM((rows_here, width), BF16),
            pltpu.VMEM((rows_here, width), BF16),
            pltpu.SemaphoreType.DMA((rows_here // BLK,)),
        ],
        60 if big else 14,
        2 * 2 * owned * width * 3 * width,
        0,
        "final",
        FAR,
    )(
        place, block_lists, own1, pair0, pair1, side0, side1, done, near_pairs,
        w_qkv, near(w_coarse_out), near(w_kv2), near(w_out), *parts,
    )


def solution(mesh):
    placed = (
        P(("coarse", "fine"), None),
        P(),
        P(),
        P(),
        P(),
        P("coarse"),
        P("coarse"),
        P(("coarse", "fine"), None),
    )
    return jax.shard_map(
        body, mesh=mesh, in_specs=placed, out_specs=P(("coarse", "fine"), None), check_vma=False
    )
```

```python
import functools
import math

import jax
import jax.numpy as jnp
from jax import lax
from jax.experimental import pallas as pl
from jax.experimental.pallas import tpu as pltpu
from jax.sharding import PartitionSpec as P

HEADS = 8
KB = 16
QB = 256
BLK = 128
MIB = 1 << 20
AXES = ("coarse", "fine")
F32 = jnp.float32
BF16 = jnp.bfloat16

VM = pl.BlockSpec(memory_space=pltpu.VMEM)
ANY = pl.BlockSpec(memory_space=pl.ANY)
FAR = pl.BlockSpec(memory_space=pltpu.HBM)


def cdiv(a, b):
    return -(-a // b)


def dot(a, b):
    return jnp.dot(a, b, preferred_element_type=F32)


def dot_t(a, b):
    return lax.dot_general(a, b, (((1,), (1,)), ((), ())), preferred_element_type=F32)


def spot():
    return lax.axis_index("coarse"), lax.axis_index("fine")


def call(kernel, outs, in_specs, scratch, limit, flops, moved, name, out_specs=None):
    return pl.pallas_call(
        kernel,
        out_shape=outs,
        in_specs=in_specs,
        out_specs=out_specs or jax.tree.map(lambda _: VM, outs),
        scratch_shapes=scratch,
        compiler_params=pltpu.CompilerParams(vmem_limit_bytes=limit * MIB),
        cost_estimate=pl.CostEstimate(flops=flops, bytes_accessed=moved, transcendentals=0),
        name=name,
    )


def sums_kernel(chunk, starts_far, ends_far, tokens_far, own, send, tokens, roots, acc, root, starts, ends, sem):
    copies = [
        pltpu.make_async_copy(source, target, sem.at[i])
        for i, (source, target) in enumerate(((starts_far, starts), (ends_far, ends), (tokens_far, tokens)))
    ]
    for copy in copies:
        copy.start()
    rows = tokens.shape[0]
    owned = starts.shape[1]
    coarse_index, fine_index = spot()
    mine = fine_index & 3
    first_row = (coarse_index * lax.axis_size("fine") + fine_index) * rows
    where_ = first_row + lax.broadcasted_iota(jnp.int32, (BLK, rows), 1)
    copies[0].wait()
    copies[1].wait()
    members = []
    for s in range(owned // BLK):
        at = slice(s * BLK, (s + 1) * BLK)
        low = jnp.broadcast_to(starts[:, at], (BLK, BLK)).T
        high = jnp.broadcast_to(ends[:, at], (BLK, BLK)).T
        root[at, :] = jnp.sqrt((high - low).astype(F32))
        low = jnp.concatenate([low] * (rows // BLK), axis=1)
        high = jnp.concatenate([high] * (rows // BLK), axis=1)
        members.append(jnp.where((where_ >= low) & (where_ < high), 1.0, 0.0).astype(BF16))
    copies[2].wait()
    for s in range(owned // BLK):
        acc[s * BLK : (s + 1) * BLK, :] = dot(members[s], tokens[...])
    own[...] = acc[pl.ds(pl.multiple_of(mine * chunk, chunk), chunk), :]
    for i, r in enumerate((0, 2)):
        roots[i * chunk : (i + 1) * chunk, :] = root[pl.ds(pl.multiple_of((mine ^ r) * chunk, chunk), chunk), :]
    for r in range(1, 4):
        theirs = pl.multiple_of((mine ^ r) * chunk, chunk)
        send[r - 1][...] = acc[pl.ds(theirs, chunk), :].astype(BF16)


def add_kernel(own, *rest):
    *got, total, half = rest
    sums = own[...]
    for cells in got:
        sums = sums + cells[...].astype(F32)
    total[...] = sums
    half[...] = sums.astype(BF16)


def pool_kernel(total, across, beside, corner, roots, pooled):
    chunk, width = total.shape
    mine = total[...] + across[...].astype(F32)
    theirs = beside[...].astype(F32) + corner[...].astype(F32)
    root = jnp.concatenate([roots[...]] * (width // BLK), axis=1)
    pooled[:chunk, :] = (mine / root[:chunk]).astype(BF16)
    pooled[chunk:, :] = (theirs / root[chunk:]).astype(BF16)


def local_kernel(first, heads, size, scale, tokens, weights, after, query, mix, level):
    del after
    width = tokens.shape[1]
    span = heads * size
    parts = [
        dot(tokens[...], weights[:, k * width + first * size : k * width + first * size + span]).astype(BF16)
        for k in range(3)
    ]
    attend_here(heads, size, scale, parts, query, mix, level)


def far_kernel(first, heads, size, scale, tokens, w_far, after, query, mix, level, weights, sem):
    del after
    width = tokens.shape[1]
    span = heads * size
    copies = []
    for k in range(3):
        at = k * width + first * size
        copies.append(pltpu.make_async_copy(w_far.at[:, at : at + span], weights.at[k], sem.at[k]))
        copies[k].start()
    parts = []
    for k in range(3):
        copies[k].wait()
        parts.append(dot(tokens[...], weights[k]).astype(BF16))
    attend_here(heads, size, scale, parts, query, mix, level)


def attend_here(heads, size, scale, parts, query, mix, level):
    queries, keys, cells = parts
    query[...] = queries
    ones = jnp.ones((keys.shape[0], size), BF16)
    for i in range(heads):
        at = slice(i * size, (i + 1) * size)
        scores = dot_t(queries[:, at], keys[:, at])
        highest = jnp.max(scores, axis=1, keepdims=True)
        expos = jnp.exp2((scores - highest) * scale).astype(BF16)
        both = dot(expos, jnp.concatenate([cells[:, at], ones], axis=1))
        total = both[:, size:]
        mix[:, at] = both[:, :size] / total
        level[:, at] = highest * scale + jnp.log2(total)


def normalize(cells):
    return cells * lax.rsqrt(jnp.mean(cells * cells, axis=1, keepdims=True) + 1e-06)


def rows_kernel(cells, w_qkv, out):
    for c in range(0, out.shape[1], 512):
        out[:, c : c + 512] = dot(cells[...], w_qkv[:, c : c + 512]).astype(BF16)


def move(chunk, cells, targets):
    for i, (target, to, columns) in enumerate(targets):
        target[pl.ds(pl.multiple_of(to, chunk), chunk), columns] = cells[i * chunk : (i + 1) * chunk, :]


def near_kernel(chunk, own1, ends0, ends1, done, w_qkv, pairs):
    width = w_qkv.shape[0]
    owned = chunk * 4
    mine = spot()[1] & 3
    cells = jnp.concatenate([own1[...], ends0[...], ends1[...]], axis=0)
    at = [(mine ^ r) * chunk for r in (1, 3)]
    at += [owned + (mine ^ r ^ 2) * chunk for r in (0, 2, 1, 3)]
    for c in range(0, 2 * width, 512):
        columns = slice(c, c + 512)
        found = dot(cells, w_qkv[:, width + c : width + c + 512]).astype(BF16)
        move(chunk, found, [(pairs, to, columns) for to in at])
    before = [mine * chunk, (mine ^ 2) * chunk]
    move(chunk, done[:, width:], [(pairs, to, slice(None)) for to in before])


def final_kernel(
    chunk, reach, size, scale, total_rows, head_groups,
    lists_far, own1, pair0, pair1, side0, side1, done, near_pairs,
    w_qkv, w_co, w_kv2, w_out, *rest,
):
    parts = len(rest) - 9
    held = [(p, i) for p, count in enumerate(head_groups) for i in range(count)]
    query, mix, level = (rest[k:parts:3] for k in range(3))
    out, far_pairs, coarse_query, mixes, listed, attended, ready, lists, sem = rest[parts:]
    lists_copy = pltpu.make_async_copy(lists_far, lists, sem.at[0])
    lists_copy.start()
    width = mixes.shape[1]
    owned = chunk * 4
    coarse_index, fine_index = spot()
    mine = fine_index & 3
    core = coarse_index & 1

    own_at = [owned + (mine ^ r) * chunk for r in (0, 2, 1, 3)]
    pair_at = [(1 - core) * owned + (mine ^ r) * chunk for r in (0, 2, 1, 3)]
    side_at = [core * owned + (mine ^ r) * chunk for r in (0, 2, 1, 3)]
    pair_to = [(1 - core) * 2 * owned + (mine ^ r) * chunk for r in (0, 2, 1, 3)]
    side_to = [core * 2 * owned + (mine ^ r) * chunk for r in (0, 2, 1, 3)]
    rows = jnp.concatenate([pair0[...], pair1[...], side0[...], side1[...], own1[...]], axis=0)
    for c in range(0, width, 512):
        found = dot(rows, w_qkv[:, c : c + 512]).astype(BF16)
        move(chunk, found, [(coarse_query, to, slice(c, c + 512)) for to in pair_to + side_to + own_at[2:]])
    rows = rows[: 8 * chunk]
    for c in range(0, 2 * width, 512):
        found = dot(rows, w_qkv[:, width + c : width + c + 512]).astype(BF16)
        move(chunk, found, [(far_pairs, to, slice(c, c + 512)) for to in pair_at + side_at])
    move(chunk, done[:, :width], [(coarse_query, to, slice(None)) for to in own_at[:2]])

    runs = (
        (near_pairs, owned, reach),
        (far_pairs, 0, owned),
        (near_pairs, 0, owned),
        (far_pairs, owned, owned),
        (near_pairs, owned + reach, reach),
    )

    def window(first, count, columns):
        cells = []
        start = 0
        for source, at, rows in runs:
            low, high = max(first, start), min(first + count, start + rows)
            if low < high:
                cells.append(source[at + low - start : at + high - start, columns])
            start += rows
        return jnp.concatenate(cells, axis=0)

    span = BLK + 2 * reach
    row = lax.broadcasted_iota(jnp.int32, (BLK, span), 0)
    column = lax.broadcasted_iota(jnp.int32, (BLK, span), 1)
    inside = (column >= row) & (column <= row + 2 * reach)
    ones = jnp.ones((span, size), BF16)
    for first in range(0, 3 * owned, BLK):
        heads = [slice(h * size, (h + 1) * size) for h in range(HEADS)]
        scores = []
        for at in heads:
            score = dot_t(coarse_query[first : first + BLK, at], window(first, span, at))
            scores.append(jnp.where(inside, score, -1e30))
        tops = [jnp.max(score, axis=1, keepdims=True) for score in scores]
        expos = [jnp.exp2((score - top) * scale).astype(BF16) for score, top in zip(scores, tops)]
        mixed = []
        for at, expo in zip(heads, expos):
            cells = window(first, span, slice(width + at.start, width + at.stop))
            both = dot(expo, jnp.concatenate([cells, ones], axis=1))
            mixed.append((both[:, :size] / both[:, size:]).astype(BF16))
        mixes[first : first + BLK, :] = jnp.concatenate(mixed, axis=1)

    groups, picks = lists.shape
    base = total_rows - (coarse_index - 1) * owned
    lists_copy.wait()
    for n in range(groups):
        for m in range(picks):
            at = pl.multiple_of(lax.rem(lists[n, m] * KB + base, total_rows), KB)
            to = (n * picks + m) * KB
            listed[to : to + KB, :] = mixes[pl.ds(at, KB), :]
    listed[...] = normalize(dot(listed[...], w_co[...])).astype(BF16)

    here = picks * KB
    ones_here = jnp.ones((here, size), BF16)
    span2 = 2 * size
    second = [
        [dot(listed[...], w_kv2[:, k * width + c : k * width + c + span2]).astype(BF16) for k in range(2)]
        for c in range(0, width, span2)
    ]

    blank = jnp.zeros((here, size), BF16)

    def fine_scores(n, pair):
        part, place_in = held[2 * pair]
        both = query[part][n * QB : (n + 1) * QB, place_in * size : (place_in + 2) * size]
        keys = second[pair][0][n * here : (n + 1) * here, :]
        first = jnp.concatenate([keys[:, :size], blank], axis=1)
        other = jnp.concatenate([blank, keys[:, size:]], axis=1)
        scores = dot_t(both, jnp.concatenate([first, other], axis=0)) * scale
        return scores[:, :here], scores[:, here:]

    def fine(n):
        scores = [c for pair in range(HEADS // 2) for c in fine_scores(n, pair)]
        rows = slice(n * QB, (n + 1) * QB)
        at = [(part, slice(i * size, (i + 1) * size)) for part, i in held]
        tops = [
            jnp.maximum(level[part][rows, columns], jnp.max(score, axis=1, keepdims=True))
            for (part, columns), score in zip(at, scores)
        ]
        boths = []
        for h in range(HEADS):
            expos = jnp.exp2(scores[h] - tops[h][:, :here]).astype(BF16)
            cells = second[h // 2][1][n * here : (n + 1) * here, h % 2 * size : (h % 2 + 1) * size]
            boths.append(dot(expos, jnp.concatenate([cells, ones_here], axis=1)))
        for h, (part, columns) in enumerate(at):
            keep = jnp.exp2(level[part][rows, columns] - tops[h])
            mixed = mix[part][rows, columns] * keep + boths[h][:, :size]
            attended[rows, h * size : (h + 1) * size] = (mixed / (keep + boths[h][:, size:])).astype(BF16)

    copies = []
    for n in range(groups):
        fine(n)
    for first in range(0, out.shape[0], BLK):
        some = slice(first, first + BLK)
        ready[some, :] = normalize(dot(attended[some, :], w_out[...])).astype(BF16)
        copies.append(pltpu.make_async_copy(ready.at[some], out.at[some], sem.at[1 + len(copies)]))
        copies[-1].start()
    for copy in copies:
        copy.wait()


def swap(cells, coarse_bit, fine_bit):
    coarse_count = lax.axis_size("coarse")
    fine_count = lax.axis_size("fine")
    pairs = [
        (c * fine_count + f, (c ^ coarse_bit) * fine_count + (f ^ fine_bit))
        for c in range(coarse_count)
        for f in range(fine_count)
    ]
    return lax.ppermute(cells, AXES, pairs)


def shift(cells, chips, fine_bit):
    coarse_count = lax.axis_size("coarse")
    fine_count = lax.axis_size("fine")
    pairs = [
        (c * fine_count + f, ((c + 2 * chips) % coarse_count) * fine_count + (f ^ fine_bit))
        for c in range(coarse_count)
        for f in range(fine_count)
    ]
    return lax.ppermute(cells, AXES, pairs)


def body(tokens, w_qkv, w_coarse_out, w_kv2, w_out, seg_start, seg_end, block_lists):
    rows_here, width = tokens.shape
    size = width // HEADS
    fine_count = lax.axis_size("fine")
    coarse_count = lax.axis_size("coarse")
    coarse_index = lax.axis_index("coarse")
    owned = seg_start.shape[0]
    chunk = owned // 4
    reach = owned // 2
    scale = math.log2(math.e) / math.sqrt(size)
    mine = lax.axis_index("fine") & 3
    big = coarse_count > 4
    far = functools.partial(pltpu.with_memory_space_constraint, memory_space=pltpu.HBM)
    kept = jax.ShapeDtypeStruct if big else pltpu.VMEM
    near = (lambda c: c) if big else functools.partial(pltpu.with_memory_space_constraint, memory_space=pltpu.VMEM)
    own, *send, tokens, roots = call(
        lambda *refs: sums_kernel(chunk, *refs[:4], refs[4:7], *refs[7:]),
        (
            jax.ShapeDtypeStruct((chunk, width), F32),
            *[jax.ShapeDtypeStruct((chunk, width), BF16)] * 3,
            kept(tokens.shape, BF16),
            jax.ShapeDtypeStruct((2 * chunk, BLK), F32),
        ),
        [FAR, FAR, FAR],
        [
            pltpu.VMEM((owned, width), F32),
            pltpu.VMEM((owned, BLK), F32),
            pltpu.VMEM((1, owned), jnp.int32),
            pltpu.VMEM((1, owned), jnp.int32),
            pltpu.SemaphoreType.DMA((3,)),
        ],
        24 if big else 8,
        2 * owned * rows_here * width,
        rows_here * width * 2,
        "sums",
    )(far(seg_start.reshape(1, owned)), far(seg_end.reshape(1, owned)), far(tokens))

    head_groups = (2, 4, 2)

    def local(first, heads, weights, after):
        span = heads * size
        results = (
            jax.ShapeDtypeStruct((rows_here, span), BF16),
            jax.ShapeDtypeStruct((rows_here, span), F32),
            jax.ShapeDtypeStruct((rows_here, span), F32),
        )
        cost = 2 * rows_here * width * 9 * size, 0, f"local{first}"
        if first == 0:
            return call(
                functools.partial(far_kernel, first, heads, size, scale),
                results,
                [VM, FAR, ANY],
                [pltpu.VMEM((3, width, span), BF16), pltpu.SemaphoreType.DMA((3,))],
                24 if big else 10,
                *cost,
            )(tokens, far(weights), after)
        kernel = functools.partial(local_kernel, first, heads, size, scale)
        return call(kernel, results, [VM, VM, ANY], [], 24 if big else 10, *cost)(tokens, weights, after)

    def beside(value, made):
        value, first = lax.optimization_barrier((value, made[0]))
        return value, [first, *made[1:]]

    got = [swap(send[r - 1], 0, r) for r in range(1, 4)]
    own, part = beside(own, local(0, 2, w_qkv, send[0]))
    parts = list(part)
    rows32 = jax.ShapeDtypeStruct((chunk, width), F32)
    rows16 = jax.ShapeDtypeStruct((chunk, width), BF16)

    def add(total, got):
        return call(
            add_kernel, (rows32, rows16), [VM] * (1 + len(got)), [], 8 if big else 4, 0, chunk * width, "add"
        )(total, *got)

    sums, half = add(own, got)
    bit = 8
    while bit < fine_count:
        sums, half = add(sums, [swap(half, 0, bit)])
        bit *= 2
    across, beside_half, corner = (swap(half, 0, bit) for bit in (4, 2, 6))
    sums, part = beside(sums, local(2, 4, w_qkv, half))
    parts.extend(part)
    own0 = call(
        pool_kernel,
        jax.ShapeDtypeStruct((2 * chunk, width), BF16),
        [VM] * 5,
        [],
        8 if big else 4,
        0,
        chunk * width,
        "pool",
    )(sums, across, beside_half, corner, roots)
    own1 = swap(own0, 0, 1)
    chips = coarse_count // 2
    core = coarse_index & 1
    if chips == 2:
        ends0 = side0 = swap(own0, 2, 0)
        ends1 = side1 = swap(own0, 2, 1)
    else:
        before0, before1 = shift(own0, 1, 0), shift(own0, 1, 1)
        after0, after1 = shift(own0, -1, 0), shift(own0, -1, 1)
        side0 = jnp.where(core == 0, after0, before0)
        side1 = jnp.where(core == 0, after1, before1)
        upper = jnp.repeat(jnp.stack([mine >= 2, mine < 2]), chunk)[:, None]
        ends0 = jnp.where(upper, before0, after0)
        ends1 = jnp.where(upper, before1, after1)
    done = call(
        rows_kernel,
        jax.ShapeDtypeStruct((2 * chunk, 3 * width), BF16),
        [VM, VM],
        [],
        40 if big else 8,
        2 * 2 * chunk * width * 3 * width,
        0,
        "rows",
    )(own0, w_qkv)
    side0, part = beside(side0, local(6, 2, w_qkv, own0))
    side0, (done,) = beside(side0, [done])
    own0 = lax.optimization_barrier((own0, side0))[0]
    parts.extend(part)
    pair0, pair1, side0, side1 = (swap(c, 1, 0) for c in (own0, own1, side0, side1))
    near_pairs = call(
        functools.partial(near_kernel, chunk),
        jax.ShapeDtypeStruct((2 * owned, 2 * width), BF16),
        [VM] * 5,
        [],
        40 if big else 8,
        2 * owned * width * 3 * width,
        0,
        "near",
    )(own1, ends0, ends1, done, w_qkv)

    listed_rows = block_lists.shape[0] * block_lists.shape[1] * KB
    return call(
        functools.partial(final_kernel, chunk, reach, size, scale, owned * coarse_count, head_groups),
        jax.ShapeDtypeStruct((rows_here, width), BF16),
        [FAR] + [VM] * (11 + len(parts)),
        [
            pltpu.VMEM((2 * owned, 2 * width), BF16),
            pltpu.VMEM((3 * owned, width), BF16),
            pltpu.VMEM((3 * owned, width), BF16),
            pltpu.VMEM((listed_rows, width), BF16),
            pltpu.VMEM((rows_here, width), BF16),
            pltpu.VMEM((rows_here, width), BF16),
            pltpu.SMEM(block_lists.shape, jnp.int32),
            pltpu.SemaphoreType.DMA((1 + rows_here // BLK,)),
        ],
        60 if big else 14,
        2 * 2 * owned * width * 3 * width,
        0,
        "final",
        FAR,
    )(
        far(block_lists), own1, pair0, pair1, side0, side1, done, near_pairs,
        w_qkv, near(w_coarse_out), near(w_kv2), near(w_out), *parts,
    )


def solution(mesh):
    placed = (
        P(("coarse", "fine"), None),
        P(),
        P(),
        P(),
        P(),
        P("coarse"),
        P("coarse"),
        P(("coarse", "fine"), None),
    )
    return jax.shard_map(
        body, mesh=mesh, in_specs=placed, out_specs=P(("coarse", "fine"), None), check_vma=False
    )
```
